256 devices in a mesh: dp: 16 (over z, core), section: 4 (over x), mp: 4 (over y).
Axes of the slice: x: 4, y: 4, z: 8, core: 2. Of those that a mesh axis runs over, the one named last changes fastest.
Arguments:
- enc_inputs: bfloat16 [4, 64, 64, 1408], P('section', 'dp'), may hold values from -6 to 6
- enc_output: bfloat16 [64, 64, 1408], P('dp'), may hold values from -6 to 6
- target_feats: bfloat16 [64, 128, 1408], P('dp', None, 'mp'), may hold values from -6 to 6
- pos_table: bfloat16 [128, 1024], replicated, may hold values from -6 to 6
- ctx_count: int32 [64], P('dp'), may hold values from 16 to 64, as said below
- tgt_index: int32 [64, 64], P('dp'), may hold values from 0 to 127, as said below
- tgt_count: int32 [64], P('dp'), may hold values from 16 to 64, as said below
- in_proj: bfloat16 [1408, 1024], P('dp'), may hold values from -0.15625 to 0.15625
- out_proj: bfloat16 [1024, 1408], P(None, 'mp'), may hold values from -0.1875 to 0.1875
- up_weight: bfloat16 [4, 1408, 6144], P('section', None, 'mp'), may hold values from -0.15625 to 0.15625
- down_weight: bfloat16 [4, 1408, 6144], P('section', None, 'mp'), may hold values from -0.078125 to 0.078125
Outputs:
- up_grad: bfloat16 [4, 1408, 6144], P('section', 'dp', 'mp')
- down_grad: bfloat16 [4, 1408, 6144], P('section', 'dp', 'mp')
- enc_grad: bfloat16 [4, 64, 64, 1408], P('section', 'dp', 'mp')
The draws below stay inside these ranges and needn't reach their ends.
Inputs may be any that keep to these rules, and one draw needn't show every extreme that they name: `ctx_count`: some clip has all 64 context slots live. `tgt_count`: some clip has all 64 target slots live. `tgt_index`: the indices of one clip are distinct.
All inputs are finite; a program needn't handle non-finite values.
Results may differ from the reference program's by a relative error of at most 0.035.
Values may be sent and summed in bfloat16 or wider, within the bound.
No kernel may reach another device: no remote copies, remote signals or barrier semaphores. Data moves between devices by JAX's collectives and lax.ppermute only.
A program may use at most 128 MiB of HBM per device.

```python
import jax
import jax.numpy as jnp
from jax import lax

D = 1408
FF = 6144
PD = 1024
MICRO = 4
ROWS = 64
LAYERS = 4
TOKS = 128
TGT = 64
MICRO_TOTAL = 64
N_DP = 16


def counts_with_full(key, most):
    first, second = jax.random.split(key)
    counts = jax.random.randint(first, (MICRO_TOTAL,), most // 4, most + 1)
    full = jax.random.randint(second, (), 0, MICRO_TOTAL)
    return jnp.where(jnp.arange(MICRO_TOTAL) == full, most, counts).astype(jnp.int32)


def draw_ctx_count(key, part):
    key = jax.random.fold_in(key, 11)
    return counts_with_full(key, ROWS)


def draw_tgt_count(key, part):
    key = jax.random.fold_in(key, 12)
    return counts_with_full(key, TGT)


def draw_tgt_index(key, part):
    key = jax.random.fold_in(key, 13)
    keys = jax.random.split(key, MICRO_TOTAL)
    picks = jax.vmap(lambda single: jax.random.permutation(single, TOKS)[:TGT])(keys)
    return picks.astype(jnp.int32)


def level_of(stream_key, shape, cuts, least, high):
    level = 1.0
    for dim, shards_of in cuts:
        heights = jax.random.uniform(jax.random.fold_in(jax.random.fold_in(stream_key, 6), dim), (shards_of,), jnp.float32, least / len(cuts), high / len(cuts))
        level = level * jnp.repeat(jnp.exp(heights), shape[dim] // shards_of).reshape((-1,) + (1,) * (len(shape) - 1 - dim))
    return level


def scatter_about(stream_key, shape, scale, bound, shards=(), kind=jnp.bfloat16):
    level = level_of(stream_key, shape, shards, -0.22, 0.18) if shards else 1.0
    array = jax.random.normal(stream_key, shape, jnp.float32) * scale * level
    return jnp.minimum(jnp.maximum(array, -bound), bound).astype(kind)


def setup_inputs(seed: int = 0) -> dict:
    key_of = jax.random.split(jax.random.key(seed), 12)
    return {
        "enc_inputs": scatter_about(key_of[0], (LAYERS, MICRO_TOTAL, ROWS, D), 1.0, 6.0, ((0, 4), (1, 16))),
        "enc_output": scatter_about(key_of[1], (MICRO_TOTAL, ROWS, D), 1.0, 6.0, ((0, 16),)),
        "target_feats": scatter_about(key_of[2], (MICRO_TOTAL, TOKS, D), 1.0, 6.0, ((0, 16), (2, 4))),
        "pos_table": scatter_about(key_of[3], (TOKS, PD), 1.0, 6.0),
        "ctx_count": draw_ctx_count(jax.random.fold_in(key_of[11], 71), 0),
        "tgt_index": draw_tgt_index(jax.random.fold_in(key_of[11], 71), 0),
        "tgt_count": draw_tgt_count(jax.random.fold_in(key_of[11], 71), 0),
        "in_proj": scatter_about(key_of[7], (D, PD), D ** -0.5, 0.15625, ((0, 16),)),
        "out_proj": scatter_about(key_of[8], (PD, D), PD ** -0.5, 0.1875, ((1, 4),)),
        "up_weight": scatter_about(key_of[9], (LAYERS, D, FF), D ** -0.5, 0.15625, ((0, 4), (2, 4))),
        "down_weight": scatter_about(key_of[10], (LAYERS, D, FF), FF ** -0.5, 0.078125, ((0, 4), (2, 4))),
    }


eps = 1e-06
loss_scale = 64.0

def gelu_exact(value):
    return jax.nn.gelu(value, approximate=False)

def normalize(inputs):
    values = inputs.astype(jnp.float32)
    centered = values - lax.optimization_barrier(jnp.mean(values, axis=-1, keepdims=True))
    rstd = lax.rsqrt(lax.optimization_barrier(jnp.mean(centered * centered, axis=-1, keepdims=True)) + eps)
    return (centered * rstd, rstd)

def norm_back(unit, rstd, dunit, upper):
    inner = dunit - lax.optimization_barrier(jnp.mean(dunit, axis=-1, keepdims=True)) - unit * lax.optimization_barrier(jnp.mean(dunit * unit, axis=-1, keepdims=True))
    return (upper.astype(jnp.float32) + rstd * inner).astype(jnp.bfloat16)

def rows_of(table, index):
    return jax.vmap(lambda block, picks: jnp.take(block, picks, axis=0))(table, index)

def block_back(up_w, down_w, inputs, upper):
    unit, rstd = normalize(inputs)
    unit_b = unit.astype(jnp.bfloat16)
    pre = jnp.dot(unit_b, up_w, preferred_element_type=jnp.float32)
    act = gelu_exact(pre).astype(jnp.bfloat16)
    dact = jnp.dot(upper, down_w, preferred_element_type=jnp.float32)
    dpre = jax.vjp(gelu_exact, pre)[1](dact)[0].astype(jnp.bfloat16)
    up_term = jnp.dot(unit_b.T, dpre, preferred_element_type=jnp.float32)
    down_term = jnp.dot(upper.T, act, preferred_element_type=jnp.float32)
    dunit = jnp.dot(dpre, up_w.T, preferred_element_type=jnp.float32)
    return (norm_back(unit, rstd, dunit, upper), up_term, down_term)

def reference(enc_inputs, enc_output, target_feats, pos_table, ctx_count, tgt_index, tgt_count, in_proj, out_proj, up_weight, down_weight):
    ctx_live = (jnp.arange(ROWS, dtype=jnp.int32)[None, :] < ctx_count[:, None]).astype(jnp.float32)
    ctx_n = ctx_count.astype(jnp.float32)
    pooled = (lax.optimization_barrier(jnp.sum(enc_output.astype(jnp.float32) * ctx_live[:, :, None], axis=1)) / ctx_n[:, None]).astype(jnp.bfloat16)
    embed = jnp.dot(pooled, in_proj, preferred_element_type=jnp.float32)
    hidden = (rows_of(jnp.broadcast_to(pos_table, (MICRO_TOTAL, TOKS, PD)), tgt_index).astype(jnp.float32) + embed[:, None, :]).astype(jnp.bfloat16)
    pred = jnp.einsum('ctp,pd->ctd', hidden.astype(jnp.float32), out_proj.astype(jnp.float32))
    target = rows_of(target_feats, tgt_index).astype(jnp.float32)
    tgt_live = (jnp.arange(TGT, dtype=jnp.int32)[None, :] < tgt_count[:, None]).astype(jnp.float32)
    dpred = loss_scale * (pred - target) * tgt_live[:, :, None] / tgt_count.astype(jnp.float32)[:, None, None]
    total = lax.optimization_barrier(jnp.sum(dpred, axis=1)).astype(jnp.bfloat16)
    dembed = jnp.dot(total, out_proj.T, preferred_element_type=jnp.float32).astype(jnp.bfloat16)
    dpooled = jnp.dot(dembed, in_proj.T, preferred_element_type=jnp.float32)
    upper = (dpooled[:, None, :] * ctx_live[:, :, None] / ctx_n[:, None, None]).astype(jnp.bfloat16)
    grads_in = [None] * LAYERS
    grads_up = [None] * LAYERS
    grads_down = [None] * LAYERS
    for layer in range(LAYERS - 1, -1, -1):
        up_w = up_weight[layer]
        down_w = down_weight[layer]
        inputs = enc_inputs[layer].reshape(N_DP, MICRO, ROWS, D)
        uppers = upper.reshape(N_DP, MICRO, ROWS, D)

        def inner(carry, pair):
            dx, up_term, down_term = block_back(up_w, down_w, pair[0], pair[1])
            return ((carry[0] + up_term, carry[1] + down_term), dx)

        def outer(carry, pair):
            zero = jnp.zeros((D, FF), jnp.float32)
            group, dxs = lax.scan(inner, (zero, zero), pair)
            up_b = lax.optimization_barrier(group[0].astype(jnp.bfloat16)).astype(jnp.float32)
            down_b = lax.optimization_barrier(group[1].astype(jnp.bfloat16)).astype(jnp.float32)
            return ((carry[0] + up_b, carry[1] + down_b), dxs)
        start = jnp.zeros((D, FF), jnp.float32)
        sums, dxs = lax.scan(outer, (start, start), (inputs, uppers))
        upper = dxs.reshape(MICRO_TOTAL, ROWS, D)
        grads_in[layer] = upper
        grads_up[layer] = sums[0].astype(jnp.bfloat16)
        grads_down[layer] = sums[1].astype(jnp.bfloat16)
    return (jnp.stack(grads_up), jnp.stack(grads_down), jnp.stack(grads_in))
```

```python
import jax
import jax.numpy as jnp
from jax import lax
from jax.sharding import PartitionSpec as P

eps = 1e-06
loss_scale = 64.0
f32 = jnp.float32
bf16 = jnp.bfloat16


def gelu_exact(value):
    return jax.nn.gelu(value, approximate=False)


def normalize(inputs):
    values = inputs.astype(f32)
    centered = values - jnp.mean(values, axis=-1, keepdims=True)
    rstd = lax.rsqrt(jnp.mean(centered * centered, axis=-1, keepdims=True) + eps)
    return (centered * rstd, rstd)


def norm_back(unit, rstd, dunit, upper):
    inner = (
        dunit
        - jnp.mean(dunit, axis=-1, keepdims=True)
        - unit * jnp.mean(dunit * unit, axis=-1, keepdims=True)
    )
    return (upper.astype(f32) + rstd * inner).astype(bf16)


def shifted(block, axis, distance):
    size = lax.axis_size(axis)
    return lax.ppermute(block, axis, [(i, (i + distance) % size) for i in range(size)])


def spread(share, axis):
    size = lax.axis_size(axis)
    return jnp.stack([share] + [shifted(share, axis, -k) for k in range(1, size)])


def scatter_sum(pieces, axis):
    size = lax.axis_size(axis)
    total = pieces[0].astype(f32)
    for k in range(1, size):
        total = total + shifted(pieces[k], axis, k).astype(f32)
    return total


def other_core(block):
    size = lax.axis_size("dp")
    return lax.ppermute(block, "dp", [(i, i ^ 1) for i in range(size)])


def next_chip(block, direction):
    size = lax.axis_size("dp")
    return lax.ppermute(block, "dp", [(i, (i + 2 * direction) % size) for i in range(size)])


def chip_scatter(blocks, direction):
    size = lax.axis_size("dp")
    chips = size // 2
    me = lax.axis_index("dp")
    chip = me // 2
    core = me % 2
    pairs = blocks.reshape((chips, 2) + blocks.shape[1:])
    theirs = lax.dynamic_index_in_dim(pairs, 1 - core, 1, keepdims=False)
    mine = lax.dynamic_index_in_dim(pairs, core, 1, keepdims=False)
    held = (mine.astype(f32) + other_core(theirs).astype(f32)).astype(bf16)

    def part(offset):
        return lax.dynamic_index_in_dim(held, (chip + offset) % chips, 0, keepdims=False)

    total = part(0).astype(f32)
    for way, reach in ((direction, chips // 2), (-direction, chips // 2 - 1)):
        moving = next_chip(part(way * reach), way)
        for left in range(reach - 1, 0, -1):
            moving = next_chip((moving.astype(f32) + part(way * left).astype(f32)).astype(bf16), way)
        total = total + moving.astype(f32)
    return total.astype(bf16)


def per_device(
    enc_inputs,
    enc_output,
    target_feats,
    pos_table,
    ctx_count,
    tgt_index,
    tgt_count,
    in_proj,
    out_proj,
    up_weight,
    down_weight,
):
    micro, rows, width = enc_output.shape
    slots = tgt_index.shape[1]
    toks = target_feats.shape[1]
    sections = lax.axis_size("section")
    section_idx = lax.axis_index("section")
    shards = lax.axis_size("mp")
    shard_idx = lax.axis_index("mp")
    share = rows // shards
    up_w = up_weight[0]
    down_w = down_weight[0]
    units = up_w.shape[1]

    both_part = jnp.dot(in_proj, out_proj, preferred_element_type=f32).astype(bf16)
    both = lax.all_gather(both_part, "dp", axis=0, tiled=True)
    ctx_n = ctx_count.astype(f32)
    tgt_n = tgt_count.astype(f32)
    ctx_live = lax.broadcasted_iota(jnp.int32, (micro, rows), 1) < ctx_count[:, None]
    pooled_sum = jnp.einsum(
        "cr,crd->cd", ctx_live.astype(bf16), enc_output, preferred_element_type=f32
    )
    pooled = (pooled_sum / ctx_n[:, None]).astype(bf16)
    tgt_live = lax.broadcasted_iota(jnp.int32, (micro, slots), 1) < tgt_count[:, None]
    hits = tgt_index[:, :, None] == lax.broadcasted_iota(jnp.int32, (micro, slots, toks), 2)
    picks = jnp.sum(jnp.where(hits & tgt_live[:, :, None], 1.0, 0.0), axis=1).astype(bf16)
    target_mean = (
        jnp.einsum("ct,ctd->cd", picks, target_feats, preferred_element_type=f32) / tgt_n[:, None]
    )
    pos_mean = jnp.dot(picks, pos_table, preferred_element_type=f32) / tgt_n[:, None]
    pos_high = pos_mean.astype(bf16)
    pos_low = (pos_mean - pos_high.astype(f32)).astype(bf16)
    pos_out = jnp.dot(
        jnp.concatenate([pos_high, pos_low]), out_proj, preferred_element_type=f32
    )
    early = pos_out[:micro] + pos_out[micro:] - target_mean
    total = loss_scale * (early + jnp.dot(pooled, both, preferred_element_type=f32))
    dpooled_part = jnp.dot(total.astype(bf16), both.T, preferred_element_type=f32)
    dpooled = dpooled_part
    for k in range(1, shards):
        dpooled = dpooled + shifted(dpooled_part, "mp", k)
    top = (dpooled / ctx_n[:, None]).astype(bf16)

    owners = (shard_idx + jnp.arange(shards)) % shards
    inputs = jnp.take(enc_inputs[0].reshape(micro, shards, share, width), owners, axis=1)
    inputs = inputs.transpose(1, 0, 2, 3).reshape(shards * micro * share, width)
    row_of = owners[:, None, None] * share + jnp.arange(share)[None, None, :]
    live = row_of < ctx_count[None, :, None]
    unit, rstd = normalize(inputs)
    unit_b = unit.astype(bf16)
    pre = jnp.dot(unit_b, up_w, preferred_element_type=f32)
    act, gelu_back = jax.vjp(gelu_exact, pre)
    act = act.astype(bf16)
    slope = gelu_back(jnp.ones_like(pre))[0]
    own = micro * share
    unit_own = unit[:own]
    rstd_own = rstd[:own]

    upper = jnp.where(live[..., None], top[None, :, None, :], jnp.zeros((), bf16))
    upper = upper.reshape(shards * own, width)
    upper_own = upper[:own]
    for step in range(sections):
        dact = jnp.dot(upper, down_w, preferred_element_type=f32)
        dpre = (dact * slope).astype(bf16)
        dunit_part = jnp.dot(dpre, up_w.T, preferred_element_type=f32).astype(bf16)
        dunit = scatter_sum(dunit_part.reshape(shards, own, width), "mp")
        dx = norm_back(unit_own, rstd_own, dunit, upper_own)
        if step + 1 < sections:
            source = sections - 1 - step
            arrived = lax.ppermute(dx, "section", [(source, source - 1)])
            upper_own = jnp.where(section_idx == source - 1, arrived, upper_own)
            upper = spread(upper_own, "mp").reshape(shards * own, width)
    down_part = jnp.einsum("rd,rf->df", upper, act, preferred_element_type=f32).astype(bf16)
    up_part = jnp.einsum("rd,rf->df", unit_b, dpre, preferred_element_type=f32).astype(bf16)
    blocks = lax.axis_size("dp")
    down_sum = chip_scatter(down_part.reshape(blocks, width // blocks, units), -1)
    up_sum = chip_scatter(up_part.reshape(blocks, width // blocks, units), 1)
    return (up_sum[None], down_sum[None], dx.reshape(1, micro, share, width))


def solution(mesh):
    return jax.shard_map(
        per_device,
        mesh=mesh,
        in_specs=(
            P("section", "dp", None, None),
            P("dp", None, None),
            P("dp", None, "mp"),
            P(),
            P("dp"),
            P("dp", None),
            P("dp"),
            P("dp", None),
            P(None, "mp"),
            P("section", None, "mp"),
            P("section", None, "mp"),
        ),
        out_specs=(
            P("section", "dp", "mp"),
            P("section", "dp", "mp"),
            P("section", "dp", "mp", None),
        ),
        check_vma=False,
    )
```

```python
import jax
import jax.numpy as jnp
from jax import lax
from jax.sharding import PartitionSpec as P

eps = 1e-06
loss_scale = 64.0
f32 = jnp.float32
bf16 = jnp.bfloat16


def gelu_and_slope(value):
    below = 0.5 + 0.5 * lax.erf(value * (0.5**0.5))
    density = jnp.exp(-0.5 * value * value) * ((2.0 * 3.141592653589793) ** -0.5)
    return (value * below, below + value * density)


def normalize(inputs):
    values = inputs.astype(f32)
    centered = values - jnp.mean(values, axis=-1, keepdims=True)
    rstd = lax.rsqrt(jnp.mean(centered * centered, axis=-1, keepdims=True) + eps)
    return (centered * rstd, rstd)


def norm_back(unit, rstd, dunit, upper):
    inner = (
        dunit
        - jnp.mean(dunit, axis=-1, keepdims=True)
        - unit * jnp.mean(dunit * unit, axis=-1, keepdims=True)
    )
    return (upper.astype(f32) + rstd * inner).astype(bf16)


def shifted(block, axis, distance):
    size = lax.axis_size(axis)
    return lax.ppermute(block, axis, [(i, (i + distance) % size) for i in range(size)])


def scatter_sum_in_steps(blocks, axis):
    size = lax.axis_size(axis)
    me = lax.axis_index(axis)

    def part(offset):
        return lax.dynamic_index_in_dim(blocks, (me + offset) % size, 0, keepdims=False)

    total = part(0).astype(f32)
    for k in range(1, size):
        total = total + shifted(part(k), axis, k).astype(f32)
    return total


def other_core(block):
    size = lax.axis_size("dp")
    return lax.ppermute(block, "dp", [(i, i ^ 1) for i in range(size)])


def next_chip(block, direction):
    size = lax.axis_size("dp")
    return lax.ppermute(block, "dp", [(i, (i + 2 * direction) % size) for i in range(size)])


def ring_pieces(blocks, way, reach):
    chips = blocks.shape[0]
    chip = lax.axis_index("dp") // 2

    def part(offset):
        return lax.dynamic_index_in_dim(blocks, (chip + offset) % chips, 0, keepdims=False)

    hops = [next_chip(part(way * reach), way)]
    for left in range(reach - 1, 0, -1):
        moving = (hops[-1].astype(f32) + part(way * left).astype(f32)).astype(bf16)
        hops.append(next_chip(moving, way))
    return hops


def chip_sum(blocks, ahead, behind):
    chips = blocks.shape[0]
    chip = lax.axis_index("dp") // 2
    own = lax.dynamic_index_in_dim(blocks, chip, 0, keepdims=False)
    return (own.astype(f32) + ahead[-1].astype(f32) + behind[-1].astype(f32)).astype(bf16)


def columns_of_core(block, core):
    half = block.shape[1] // 2
    return lax.dynamic_slice_in_dim(block, core * half, half, 1)


def rows_of_both(total):
    core = lax.axis_index("dp") % 2
    rows = total.shape[0] // 2
    mine = lax.dynamic_slice_in_dim(total, core * rows, rows, 0)
    theirs = other_core(lax.dynamic_slice_in_dim(total, (1 - core) * rows, rows, 0))
    return jnp.where(
        core == 0,
        jnp.concatenate([mine, theirs], axis=1),
        jnp.concatenate([theirs, mine], axis=1),
    )


def per_device(
    enc_inputs,
    enc_output,
    target_feats,
    pos_table,
    ctx_count,
    tgt_index,
    tgt_count,
    in_proj,
    out_proj,
    up_weight,
    down_weight,
):
    micro, rows, width = enc_output.shape
    slots = tgt_index.shape[1]
    toks = target_feats.shape[1]
    sections = lax.axis_size("section")
    section_idx = lax.axis_index("section")
    shards = lax.axis_size("mp")
    shard_idx = lax.axis_index("mp")
    share = rows // shards
    one = lax.optimization_barrier(jnp.ones((), bf16))
    up_w, down_w = lax.optimization_barrier((up_weight[0] * one, down_weight[0] * one))
    units = up_w.shape[1]

    both_part = jnp.dot(in_proj, out_proj, preferred_element_type=f32).astype(bf16)
    both = lax.all_gather(both_part, "dp", axis=0, tiled=True)
    ctx_n = ctx_count.astype(f32)
    tgt_n = tgt_count.astype(f32)
    ctx_live = lax.broadcasted_iota(jnp.int32, (micro, rows), 1) < ctx_count[:, None]
    pooled_sum = jnp.einsum(
        "cr,crd->cd", ctx_live.astype(bf16), enc_output, preferred_element_type=f32
    )
    pooled = (pooled_sum / ctx_n[:, None]).astype(bf16)
    tgt_live = lax.broadcasted_iota(jnp.int32, (micro, slots), 1) < tgt_count[:, None]
    hits = tgt_index[:, :, None] == lax.broadcasted_iota(jnp.int32, (micro, slots, toks), 2)
    picks = jnp.sum(jnp.where(hits & tgt_live[:, :, None], 1.0, 0.0), axis=1).astype(bf16)
    target_mean = (
        jnp.einsum("ct,ctd->cd", picks, target_feats, preferred_element_type=f32) / tgt_n[:, None]
    )
    pos_mean = jnp.dot(picks, pos_table, preferred_element_type=f32) / tgt_n[:, None]
    pos_high = pos_mean.astype(bf16)
    pos_low = (pos_mean - pos_high.astype(f32)).astype(bf16)
    pos_out = jnp.dot(
        jnp.concatenate([pos_high, pos_low]), out_proj, preferred_element_type=f32
    )
    early = pos_out[:micro] + pos_out[micro:] - target_mean
    total = loss_scale * (early + jnp.dot(pooled, both, preferred_element_type=f32))
    dpooled_part = jnp.dot(total.astype(bf16), both.T, preferred_element_type=f32)
    dpooled = dpooled_part
    for k in range(1, shards):
        dpooled = dpooled + shifted(dpooled_part, "mp", k)
    top = (dpooled / ctx_n[:, None]).astype(bf16)

    own = micro * share
    inputs = enc_inputs[0].reshape(micro, shards, share, width)
    inputs = inputs.transpose(1, 0, 2, 3).reshape(shards * own, width)
    row_of = jnp.arange(shards)[:, None, None] * share + jnp.arange(share)[None, None, :]
    live = row_of < ctx_count[None, :, None]
    unit, rstd = normalize(inputs)
    unit_b = unit.astype(bf16)
    pre = jnp.dot(unit_b, up_w, preferred_element_type=f32)
    act, slope = gelu_and_slope(pre)
    act = act.astype(bf16)
    slope = slope.astype(bf16)
    unit_own = lax.dynamic_slice_in_dim(unit, shard_idx * own, own, 0)
    rstd_own = lax.dynamic_slice_in_dim(rstd, shard_idx * own, own, 0)

    core = lax.axis_index("dp") % 2
    unit_all = jnp.concatenate([unit_b, other_core(unit_b)])
    act_all = jnp.concatenate(
        [columns_of_core(act, core), other_core(columns_of_core(act, 1 - core))]
    )
    slope_all = jnp.concatenate(
        [columns_of_core(slope, core), other_core(columns_of_core(slope, 1 - core))]
    )
    up_half = columns_of_core(up_weight[0], core)
    down_half = columns_of_core(down_weight[0], core)

    upper = jnp.where(live[..., None], top[None, :, None, :], jnp.zeros((), bf16))
    upper = upper.reshape(shards * own, width)
    upper_own = lax.dynamic_slice_in_dim(upper, shard_idx * own, own, 0)
    for step in range(sections - 1):
        dact = jnp.dot(upper, down_w, preferred_element_type=f32)
        dpre = lax.optimization_barrier((dact * slope).astype(bf16))
        dunit_part = jnp.dot(dpre, up_w.T, preferred_element_type=f32).astype(bf16)
        dunit = scatter_sum_in_steps(dunit_part.reshape(shards, own, width), "mp")
        dx = norm_back(unit_own, rstd_own, dunit, upper_own)
        source = sections - 1 - step
        arrived = lax.ppermute(dx, "section", [(source, source - 1)])
        upper_own = jnp.where(section_idx == source - 1, arrived, upper_own)
        upper = lax.all_gather(upper_own, "mp", axis=0, tiled=True)

    chips = lax.axis_size("dp") // 2
    upper_all = lax.optimization_barrier(jnp.concatenate([upper, other_core(upper)]))
    dact = jnp.dot(upper_all, down_half, preferred_element_type=f32)
    dpre_all = lax.optimization_barrier((dact * slope_all).astype(bf16))
    down_part = jnp.einsum("rd,rf->df", upper_all, act_all, preferred_element_type=f32)
    down_part = down_part.astype(bf16).reshape(chips, width // chips, units // 2)
    up_part = jnp.einsum("rd,rf->df", unit_all, dpre_all, preferred_element_type=f32)
    up_part = up_part.astype(bf16).reshape(chips, width // chips, units // 2)
    down_part, up_part = lax.optimization_barrier((down_part, up_part))
    down_hops = (
        ring_pieces(down_part, -1, chips // 2),
        ring_pieces(down_part, 1, chips // 2 - 1),
    )
    up_hops = (
        ring_pieces(up_part, 1, chips // 2),
        ring_pieces(up_part, -1, chips // 2 - 1),
    )
    dpre_all, down_hops[0][0] = lax.optimization_barrier((dpre_all, down_hops[0][0]))
    dunit_part = jnp.dot(dpre_all, up_half.T, preferred_element_type=f32).astype(bf16)
    dunit_part = dunit_part.reshape(2, shards, own, width)
    dunit_part = (dunit_part[0].astype(f32) + other_core(dunit_part[1]).astype(f32)).astype(bf16)
    dunit = scatter_sum_in_steps(dunit_part, "mp")
    dx = norm_back(unit_own, rstd_own, dunit, upper_own)
    down_sum = rows_of_both(chip_sum(down_part, *down_hops))
    up_sum = rows_of_both(chip_sum(up_part, *up_hops))
    return (up_sum[None], down_sum[None], dx.reshape(1, micro, share, width))


def solution(mesh):
    return jax.shard_map(
        per_device,
        mesh=mesh,
        in_specs=(
            P("section", "dp", None, None),
            P("dp", None, None),
            P("dp", None, "mp"),
            P(),
            P("dp"),
            P("dp", None),
            P("dp"),
            P("dp", None),
            P(None, "mp"),
            P("section", None, "mp"),
            P("section", None, "mp"),
        ),
        out_specs=(
            P("section", "dp", "mp"),
            P("section", "dp", "mp"),
            P("section", "dp", "mp", None),
        ),
        check_vma=False,
    )
```

```python
import jax
import jax.numpy as jnp
from jax import lax
from jax.experimental import pallas as pl
from jax.experimental.pallas import tpu as pltpu
from jax.sharding import PartitionSpec as P

eps = 1e-06
loss_scale = 64.0
f32 = jnp.float32
bf16 = jnp.bfloat16


def gelu_and_slope(value):
    below = 0.5 + 0.5 * lax.erf(value * (0.5**0.5))
    density = jnp.exp(-0.5 * value * value) * ((2.0 * 3.141592653589793) ** -0.5)
    return (value * below, below + value * density)


def normalize(inputs):
    values = inputs.astype(f32)
    centered = values - jnp.mean(values, axis=-1, keepdims=True)
    rstd = lax.rsqrt(jnp.mean(centered * centered, axis=-1, keepdims=True) + eps)
    return (centered * rstd, rstd)


def norm_back(unit, rstd, dunit, upper):
    inner = (
        dunit
        - jnp.mean(dunit, axis=-1, keepdims=True)
        - unit * jnp.mean(dunit * unit, axis=-1, keepdims=True)
    )
    return (upper.astype(f32) + rstd * inner).astype(bf16)


def shifted(block, axis, distance):
    size = lax.axis_size(axis)
    return lax.ppermute(block, axis, [(i, (i + distance) % size) for i in range(size)])


def scattered(blocks, axis):
    size = lax.axis_size(axis)
    me = lax.axis_index(axis)

    def part(offset):
        return lax.dynamic_index_in_dim(blocks, (me + offset) % size, 0, keepdims=False)

    return [part(0)] + [shifted(part(k), axis, k) for k in range(1, size)]


def sum_of(blocks):
    total = blocks[0].astype(f32)
    for block in blocks[1:]:
        total = total + block.astype(f32)
    return total


def other_core(block):
    size = lax.axis_size("dp")
    return lax.ppermute(block, "dp", [(i, i ^ 1) for i in range(size)])


def next_chip(block, direction):
    size = lax.axis_size("dp")
    return lax.ppermute(block, "dp", [(i, (i + 2 * direction) % size) for i in range(size)])


def from_here(blocks):
    chips = blocks.shape[0]
    chip = lax.axis_index("dp") // 2
    return [
        lax.dynamic_index_in_dim(blocks, (chip + k) % chips, 0, keepdims=False)
        for k in range(chips)
    ]


def passed_on(moving, block, way):
    return next_chip((moving.astype(f32) + block.astype(f32)).astype(bf16), way)


def fetch_kernel(source_ref, out_ref):
    pltpu.sync_copy(source_ref, out_ref)


def fetched(weight):
    return pl.pallas_call(
        fetch_kernel,
        in_specs=[pl.BlockSpec(memory_space=pltpu.HBM)],
        out_specs=pl.BlockSpec(memory_space=pltpu.VMEM),
        out_shape=pltpu.VMEM(weight.shape, weight.dtype),
        compiler_params=pltpu.CompilerParams(vmem_limit_bytes=1024 * 1024),
        cost_estimate=pl.CostEstimate(
            flops=0, bytes_accessed=4 * weight.size, transcendentals=0
        ),
    )(weight)


def after(value, *others):
    return lax.optimization_barrier((value, *others))[0]


def tied(*values):
    return lax.optimization_barrier(values)


def columns_of_core(block, core):
    half = block.shape[1] // 2
    return lax.dynamic_slice_in_dim(block, core * half, half, 1)


def rows_of_both(total):
    core = lax.axis_index("dp") % 2
    rows = total.shape[0] // 2
    mine = lax.dynamic_slice_in_dim(total, core * rows, rows, 0)
    theirs = other_core(lax.dynamic_slice_in_dim(total, (1 - core) * rows, rows, 0))
    return jnp.where(
        core == 0,
        jnp.concatenate([mine, theirs], axis=1),
        jnp.concatenate([theirs, mine], axis=1),
    )


def per_device(
    enc_inputs,
    enc_output,
    target_feats,
    pos_table,
    ctx_count,
    tgt_index,
    tgt_count,
    in_proj,
    out_proj,
    up_weight,
    down_weight,
):
    micro, rows, width = enc_output.shape
    slots = tgt_index.shape[1]
    toks = target_feats.shape[1]
    sections = lax.axis_size("section")
    section_idx = lax.axis_index("section")
    shards = lax.axis_size("mp")
    shard_idx = lax.axis_index("mp")
    share = rows // shards
    up_w = up_weight[0]
    down_w = down_weight[0]
    units = up_w.shape[1]

    both_part = jnp.dot(in_proj, out_proj, preferred_element_type=f32).astype(bf16)
    both = lax.all_gather(both_part, "dp", axis=0, tiled=True)
    counts = lax.optimization_barrier(jnp.stack([ctx_count, tgt_count]))
    ctx_count = counts[0]
    tgt_count = counts[1]
    ctx_n = ctx_count.astype(f32)
    tgt_n = tgt_count.astype(f32)
    ctx_live = lax.broadcasted_iota(jnp.int32, (micro, rows), 1) < ctx_count[:, None]
    pooled_sum = jnp.einsum(
        "cr,crd->cd", ctx_live.astype(bf16), enc_output, preferred_element_type=f32
    )
    pooled = (pooled_sum / ctx_n[:, None]).astype(bf16)
    tgt_live = lax.broadcasted_iota(jnp.int32, (micro, slots), 1) < tgt_count[:, None]
    hits = tgt_index[:, :, None] == lax.broadcasted_iota(jnp.int32, (micro, slots, toks), 2)
    picks = jnp.sum(jnp.where(hits & tgt_live[:, :, None], 1.0, 0.0), axis=1).astype(bf16)
    target_mean = (
        jnp.einsum("ct,ctd->cd", picks, target_feats, preferred_element_type=f32) / tgt_n[:, None]
    )
    pos_mean = jnp.dot(picks, pos_table, preferred_element_type=f32) / tgt_n[:, None]
    pos_high = pos_mean.astype(bf16)
    pos_low = (pos_mean - pos_high.astype(f32)).astype(bf16)
    pos_out = jnp.dot(
        jnp.concatenate([pos_high, pos_low]), out_proj, preferred_element_type=f32
    )
    known = pos_out[:micro] + pos_out[micro:] - target_mean
    total = loss_scale * (known + jnp.dot(pooled, both, preferred_element_type=f32))
    dpooled_part = jnp.dot(total.astype(bf16), both.T, preferred_element_type=f32)
    dpooled = dpooled_part
    for k in range(1, shards):
        dpooled = dpooled + shifted(dpooled_part, "mp", k)
    top = (dpooled / ctx_n[:, None]).astype(bf16)

    own = micro * share
    inputs = enc_inputs[0].reshape(micro, shards, share, width)
    inputs = inputs.transpose(1, 0, 2, 3).reshape(shards * own, width)
    row_of = jnp.arange(shards)[:, None, None] * share + jnp.arange(share)[None, None, :]
    live = row_of < ctx_count[None, :, None]
    unit, rstd = normalize(inputs)
    unit_b = unit.astype(bf16)
    pre = jnp.dot(unit_b, up_w, preferred_element_type=f32)
    act, slope = gelu_and_slope(pre)
    act = act.astype(bf16)
    slope = slope.astype(bf16)
    unit_own = lax.dynamic_slice_in_dim(unit, shard_idx * own, own, 0)
    rstd_own = lax.dynamic_slice_in_dim(rstd, shard_idx * own, own, 0)

    core = lax.axis_index("dp") % 2
    upper = jnp.where(live[..., None], top[None, :, None, :], jnp.zeros((), bf16))
    upper = upper.reshape(shards * own, width)
    upper_own = lax.dynamic_slice_in_dim(upper, shard_idx * own, own, 0)
    other_unit = other_core(unit_b)
    last = []
    down_near = down_w
    for step in range(sections - 1):
        dact = jnp.dot(upper, down_near, preferred_element_type=f32)
        dpre = lax.optimization_barrier((dact * slope).astype(bf16))
        dunit_part = jnp.dot(dpre, up_w.T, preferred_element_type=f32).astype(bf16)
        parts = scattered(dunit_part.reshape(shards, own, width), "mp")
        if step == 0:
            last = [
                jnp.concatenate([unit_b, other_unit]),
                *[columns_of_core(x, c) for x in tied(act, slope) for c in (core, 1 - core)],
            ]
        if step == 1:
            last = [last[0], jnp.concatenate(last[1:3]), jnp.concatenate(last[3:5])]
            last = last + [columns_of_core(up_w, core)]
        if step == 2:
            last = last + [columns_of_core(down_w, core)]
        else:
            down_near = fetched(after(down_w, dunit_part))
        parts, last, down_near = tied(parts, last, down_near)
        dx = norm_back(unit_own, rstd_own, sum_of(parts), upper_own)
        source = sections - 1 - step
        arrived = lax.ppermute(dx, "section", [(source, source - 1)])
        if step == 0:
            last[2] = other_core(last[2])
            last[4] = other_core(last[4])
        upper_own = jnp.where(section_idx == source - 1, arrived, upper_own)
        upper = lax.all_gather(upper_own, "mp", axis=0, tiled=True)
    unit_all, act_all, slope_all, up_half, down_half = last

    chips = lax.axis_size("dp") // 2
    half = chips // 2
    block = (chips, width // chips, units // 2)
    upper_all = lax.optimization_barrier(jnp.concatenate([upper, other_core(upper)]))
    dact = jnp.dot(upper_all, down_half, preferred_element_type=f32)
    dpre_all = lax.optimization_barrier((dact * slope_all).astype(bf16))
    down_part = jnp.einsum("rd,rf->df", upper_all, act_all, preferred_element_type=f32)
    up_part = jnp.einsum("rd,rf->df", unit_all, dpre_all, preferred_element_type=f32)
    down_blocks, up_blocks = tied(
        from_here(down_part.astype(bf16).reshape(block)),
        from_here(up_part.astype(bf16).reshape(block)),
    )
    streams = [
        (down_blocks, -1, half),
        (up_blocks, 1, half),
        (down_blocks, 1, half - 1),
        (up_blocks, -1, half - 1),
    ]
    hops = [next_chip(blocks[way * reach], way) for blocks, way, reach in streams]
    dunit_part = jnp.dot(dpre_all, up_half.T, preferred_element_type=f32).astype(bf16)
    dunit_part = dunit_part.reshape(2, shards, own, width)
    before = dunit_part
    dunit_part = (dunit_part[0].astype(f32) + other_core(dunit_part[1]).astype(f32)).astype(bf16)
    for hop in range(1, half):
        for i, (blocks, way, reach) in enumerate(streams):
            if hop < reach:
                moving = after(hops[i], before)
                before = moving.astype(f32) + blocks[way * (reach - hop)].astype(f32)
                before = before.astype(bf16)
                hops[i] = next_chip(before, way)
        if hop == 1:
            parts = scattered(after(dunit_part, before), "mp")
            before = parts[0]
    parts = list(after((*parts,), before))
    dx = norm_back(unit_own, rstd_own, sum_of(parts), upper_own)
    down_sum = rows_of_both(sum_of([down_blocks[0], hops[0], hops[2]]).astype(bf16))
    up_sum = rows_of_both(sum_of([up_blocks[0], hops[1], hops[3]]).astype(bf16))
    return (up_sum[None], down_sum[None], dx.reshape(1, micro, share, width))


def solution(mesh):
    return jax.shard_map(
        per_device,
        mesh=mesh,
        in_specs=(
            P("section", "dp", None, None),
            P("dp", None, None),
            P("dp", None, "mp"),
            P(),
            P("dp"),
            P("dp", None),
            P("dp"),
            P("dp", None),
            P(None, "mp"),
            P("section", None, "mp"),
            P("section", None, "mp"),
        ),
        out_specs=(
            P("section", "dp", "mp"),
            P("section", "dp", "mp"),
            P("section", "dp", "mp", None),
        ),
        check_vma=False,
    )
```

```python
import jax
import jax.numpy as jnp
from jax import lax
from jax.experimental import pallas as pl
from jax.experimental.pallas import tpu as pltpu
from jax.sharding import PartitionSpec as P

eps = 1e-06
loss_scale = 64.0
f32 = jnp.float32
bf16 = jnp.bfloat16


def gelu_and_slope(value):
    below = 0.5 + 0.5 * lax.erf(value * (0.5**0.5))
    density = jnp.exp(-0.5 * value * value) * ((2.0 * 3.141592653589793) ** -0.5)
    return (value * below, below + value * density)


def normalize(inputs):
    values = inputs.astype(f32)
    centered = values - jnp.mean(values, axis=-1, keepdims=True)
    rstd = lax.rsqrt(jnp.mean(centered * centered, axis=-1, keepdims=True) + eps)
    return (centered * rstd, rstd)


def norm_back(unit, rstd, dunit, upper):
    inner = (
        dunit
        - jnp.mean(dunit, axis=-1, keepdims=True)
        - unit * jnp.mean(dunit * unit, axis=-1, keepdims=True)
    )
    return (upper.astype(f32) + rstd * inner).astype(bf16)


def shifted(block, axis, distance):
    size = lax.axis_size(axis)
    return lax.ppermute(block, axis, [(i, (i + distance) % size) for i in range(size)])


def scattered(blocks, axis):
    size = lax.axis_size(axis)
    me = lax.axis_index(axis)

    def part(offset):
        return lax.dynamic_index_in_dim(blocks, (me + offset) % size, 0, keepdims=False)

    return [part(0)] + [shifted(part(k), axis, k) for k in range(1, size)]


def sum_of(blocks):
    total = blocks[0].astype(f32)
    for block in blocks[1:]:
        total = total + block.astype(f32)
    return total


def other_core(block):
    size = lax.axis_size("dp")
    return lax.ppermute(block, "dp", [(i, i ^ 1) for i in range(size)])


def next_chip(block, direction):
    size = lax.axis_size("dp")
    return lax.ppermute(block, "dp", [(i, (i + 2 * direction) % size) for i in range(size)])


def from_here(blocks):
    chips = blocks.shape[0]
    chip = lax.axis_index("dp") // 2
    return [
        lax.dynamic_index_in_dim(blocks, (chip + k) % chips, 0, keepdims=False)
        for k in range(chips)
    ]


def passed_on(moving, block, way):
    return next_chip((moving.astype(f32) + block.astype(f32)).astype(bf16), way)


copies = 8


def start_copies(source_ref, out_ref, sems):
    rows = source_ref.shape[0] // copies
    started = []
    for i in range(copies):
        part = pl.ds(i * rows, rows)
        copy = pltpu.make_async_copy(source_ref.at[part], out_ref.at[part], sems.at[i])
        copy.start()
        started.append(copy)
    return started


def fetch_kernel(source_ref, out_ref, sems):
    for copy in start_copies(source_ref, out_ref, sems):
        copy.wait()


def fetched(weight):
    return pl.pallas_call(
        fetch_kernel,
        in_specs=[pl.BlockSpec(memory_space=pltpu.HBM)],
        out_specs=pl.BlockSpec(memory_space=pltpu.VMEM),
        out_shape=pltpu.VMEM(weight.shape, weight.dtype),
        scratch_shapes=[pltpu.SemaphoreType.DMA((copies,))],
        compiler_params=pltpu.CompilerParams(vmem_limit_bytes=1024 * 1024),
        cost_estimate=pl.CostEstimate(
            flops=0, bytes_accessed=4 * weight.size, transcendentals=0
        ),
    )(pltpu.with_memory_space_constraint(weight, pltpu.HBM))


def few_rows_kernel(rows_ref, weight_ref, out_ref, held_ref, sems):
    rows = weight_ref.shape[0] // copies
    total = jnp.zeros(out_ref.shape, f32)
    for i, copy in enumerate(start_copies(weight_ref, held_ref, sems)):
        copy.wait()
        part = pl.ds(i * rows, rows)
        total = total + lax.dot_general(
            rows_ref[part, :],
            held_ref[part, :],
            (((0,), (0,)), ((), ())),
            preferred_element_type=f32,
        )
    out_ref[...] = total


def few_rows_product(rows, weight):
    few, depth = rows.shape
    cols = weight.shape[1]
    padded = jnp.pad(rows, ((0, -few % 16), (0, 0))).T
    vmem = pl.BlockSpec(memory_space=pltpu.VMEM)
    out = pl.pallas_call(
        few_rows_kernel,
        in_specs=[vmem, pl.BlockSpec(memory_space=pltpu.HBM)],
        out_specs=vmem,
        out_shape=jax.ShapeDtypeStruct((padded.shape[1], cols), f32),
        scratch_shapes=[
            pltpu.VMEM(weight.shape, weight.dtype),
            pltpu.SemaphoreType.DMA((copies,)),
        ],
        compiler_params=pltpu.CompilerParams(vmem_limit_bytes=8 * 1024 * 1024),
        cost_estimate=pl.CostEstimate(
            flops=2 * few * weight.size, bytes_accessed=2 * weight.size, transcendentals=0
        ),
    )(padded, pltpu.with_memory_space_constraint(weight, pltpu.HBM))
    return out[:few]


def after(value, *others):
    return lax.optimization_barrier((value, *others))[0]


def tied(*values):
    return lax.optimization_barrier(values)


def columns_of_core(block, core):
    half = block.shape[1] // 2
    return lax.dynamic_slice_in_dim(block, core * half, half, 1)


def rows_of_both(total):
    core = lax.axis_index("dp") % 2
    rows = total.shape[0] // 2
    mine = lax.dynamic_slice_in_dim(total, core * rows, rows, 0)
    theirs = other_core(lax.dynamic_slice_in_dim(total, (1 - core) * rows, rows, 0))
    return jnp.where(
        core == 0,
        jnp.concatenate([mine, theirs], axis=1),
        jnp.concatenate([theirs, mine], axis=1),
    )


def per_device(
    enc_inputs,
    enc_output,
    target_feats,
    pos_table,
    ctx_count,
    tgt_index,
    tgt_count,
    in_proj,
    out_proj,
    up_weight,
    down_weight,
):
    micro, rows, width = enc_output.shape
    slots = tgt_index.shape[1]
    toks = target_feats.shape[1]
    sections = lax.axis_size("section")
    section_idx = lax.axis_index("section")
    shards = lax.axis_size("mp")
    shard_idx = lax.axis_index("mp")
    share = rows // shards
    up_w = up_weight[0]
    down_w = down_weight[0]
    units = up_w.shape[1]

    both_part = jnp.dot(in_proj, out_proj, preferred_element_type=f32).astype(bf16)
    both = lax.all_gather(both_part, "dp", axis=0, tiled=True)
    counts = lax.optimization_barrier(jnp.stack([ctx_count, tgt_count]))
    ctx_count = counts[0]
    tgt_count = counts[1]
    ctx_n = ctx_count.astype(f32)
    tgt_n = tgt_count.astype(f32)
    ctx_live = lax.broadcasted_iota(jnp.int32, (micro, rows), 1) < ctx_count[:, None]
    pooled_sum = jnp.einsum(
        "cr,crd->cd", ctx_live.astype(bf16), enc_output, preferred_element_type=f32
    )
    pooled = (pooled_sum / ctx_n[:, None]).astype(bf16)
    tgt_live = lax.broadcasted_iota(jnp.int32, (micro, slots), 1) < tgt_count[:, None]
    hits = tgt_index[:, :, None] == lax.broadcasted_iota(jnp.int32, (micro, slots, toks), 2)
    picks = jnp.sum(jnp.where(hits & tgt_live[:, :, None], 1.0, 0.0), axis=1).astype(bf16)
    target_mean = (
        jnp.einsum("ct,ctd->cd", picks, target_feats, preferred_element_type=f32) / tgt_n[:, None]
    )
    pos_mean = jnp.dot(picks, pos_table, preferred_element_type=f32) / tgt_n[:, None]
    pos_high = pos_mean.astype(bf16)
    pos_low = (pos_mean - pos_high.astype(f32)).astype(bf16)
    pos_out = jnp.dot(
        jnp.concatenate([pos_high, pos_low]), out_proj, preferred_element_type=f32
    )
    known = pos_out[:micro] + pos_out[micro:] - target_mean
    total = loss_scale * (known + jnp.dot(pooled, both, preferred_element_type=f32))
    dpooled_part = jnp.dot(total.astype(bf16), both.T, preferred_element_type=f32)
    dpooled_parts = [dpooled_part] + [shifted(dpooled_part, "mp", k) for k in range(1, shards)]

    own = micro * share
    inputs = enc_inputs[0].reshape(micro, shards, share, width)
    inputs = inputs.transpose(1, 0, 2, 3).reshape(shards * own, width)
    inputs = lax.optimization_barrier(inputs)
    row_of = jnp.arange(shards)[:, None, None] * share + jnp.arange(share)[None, None, :]
    live = row_of < ctx_count[None, :, None]
    unit_b = normalize(inputs)[0].astype(bf16)
    pre = jnp.dot(unit_b, up_w, preferred_element_type=f32)
    act, slope = gelu_and_slope(pre)
    act = act.astype(bf16)
    slope = slope.astype(bf16)
    dpooled_parts, act, slope = tied(dpooled_parts, act, slope)
    top = (sum_of(dpooled_parts) / ctx_n[:, None]).astype(bf16)
    near = lax.dynamic_slice_in_dim(inputs, shard_idx * own, own, 0)
    near = normalize(lax.optimization_barrier(near))

    core = lax.axis_index("dp") % 2
    upper = jnp.where(live[..., None], top[None, :, None, :], jnp.zeros((), bf16))
    upper = upper.reshape(shards * own, width)
    upper_own = lax.dynamic_slice_in_dim(upper, shard_idx * own, own, 0)
    other_unit = other_core(unit_b)
    last = []
    for step in range(sections - 1):
        if step == 0:
            dact = few_rows_product(top, down_w)
            dact = jnp.where(live[..., None], dact[None, :, None, :], 0.0)
            dact = dact.reshape(shards * own, units)
        else:
            dact = jnp.dot(upper, down_near, preferred_element_type=f32)
        dpre = lax.optimization_barrier((dact * slope).astype(bf16))
        dunit_part = jnp.dot(dpre, up_w.T, preferred_element_type=f32).astype(bf16)
        parts = scattered(dunit_part.reshape(shards, own, width), "mp")
        if step == 0:
            last = [
                jnp.concatenate([unit_b, other_unit]),
                *[columns_of_core(x, c) for x in after((act, slope), dunit_part) for c in (core, 1 - core)],
            ]
        if step == 1:
            last = [last[0], jnp.concatenate(last[1:3]), jnp.concatenate(last[3:5])]
            last = last + [columns_of_core(up_w, core)]
        if step == 2:
            last = last + [columns_of_core(down_w, core)]
        parts, last, near = tied(parts, last, near)
        dx = norm_back(*near, sum_of(parts), upper_own)
        source = sections - 1 - step
        arrived = lax.ppermute(dx, "section", [(source, source - 1)])
        down_near = down_w
        if step == 1:
            down_near = fetched(after(down_w, dx))
            arrived, down_near = tied(arrived, down_near)
        if step == 0:
            last[2] = other_core(last[2])
            last[4] = other_core(last[4])
        upper_own = jnp.where(section_idx == source - 1, arrived, upper_own)
        upper = lax.all_gather(upper_own, "mp", axis=0, tiled=True)
    unit_all, act_all, slope_all, up_half, down_half = last

    chips = lax.axis_size("dp") // 2
    half = chips // 2
    block = (chips, width // chips, units // 2)
    upper_all = lax.optimization_barrier(jnp.concatenate([upper, other_core(upper)]))
    dact = jnp.dot(upper_all, down_half, preferred_element_type=f32)
    dpre_all = lax.optimization_barrier((dact * slope_all).astype(bf16))
    down_part = jnp.einsum("rd,rf->df", upper_all, act_all, preferred_element_type=f32)
    up_part = jnp.einsum("rd,rf->df", unit_all, dpre_all, preferred_element_type=f32)
    down_blocks, up_blocks = tied(
        from_here(down_part.astype(bf16).reshape(block)),
        from_here(up_part.astype(bf16).reshape(block)),
    )
    streams = [
        (down_blocks, -1, half),
        (up_blocks, 1, half),
        (down_blocks, 1, half - 1),
        (up_blocks, -1, half - 1),
    ]
    hops = [next_chip(blocks[way * reach], way) for blocks, way, reach in streams]
    dpre_all = after(dpre_all, down_blocks, up_blocks)
    dunit_part = jnp.dot(dpre_all, up_half.T, preferred_element_type=f32).astype(bf16)
    dunit_part = dunit_part.reshape(2, shards, own, width)
    before = dunit_part
    dunit_part = (dunit_part[0].astype(f32) + other_core(dunit_part[1]).astype(f32)).astype(bf16)
    for hop in range(1, half):
        for i, (blocks, way, reach) in enumerate(streams):
            if hop < reach:
                moving = after(hops[i], before)
                before = moving.astype(f32) + blocks[way * (reach - hop)].astype(f32)
                before = before.astype(bf16)
                hops[i] = next_chip(before, way)
        if hop == 1:
            parts = scattered(after(dunit_part, before), "mp")
            before = parts[0]
    parts = list(after((*parts,), before))
    dx = norm_back(*near, sum_of(parts), upper_own)
    down_sum = rows_of_both(sum_of([down_blocks[0], hops[0], hops[2]]).astype(bf16))
    up_sum = rows_of_both(sum_of([up_blocks[0], hops[1], hops[3]]).astype(bf16))
    return (up_sum[None], down_sum[None], dx.reshape(1, micro, share, width))


def solution(mesh):
    return jax.shard_map(
        per_device,
        mesh=mesh,
        in_specs=(
            P("section", "dp", None, None),
            P("dp", None, None),
            P("dp", None, "mp"),
            P(),
            P("dp"),
            P("dp", None),
            P("dp"),
            P("dp", None),
            P(None, "mp"),
            P("section", None, "mp"),
            P("section", None, "mp"),
        ),
        out_specs=(
            P("section", "dp", "mp"),
            P("section", "dp", "mp"),
            P("section", "dp", "mp", None),
        ),
        check_vma=False,
    )
```

```python
import jax
import jax.numpy as jnp
from jax import lax
from jax.experimental import pallas as pl
from jax.experimental.pallas import tpu as pltpu
from jax.sharding import PartitionSpec as P

eps = 1e-06
loss_scale = 64.0
f32 = jnp.float32
bf16 = jnp.bfloat16


def gelu_and_slope(value):
    below = 0.5 + 0.5 * lax.erf(value * (0.5**0.5))
    density = jnp.exp(-0.5 * value * value) * ((2.0 * 3.141592653589793) ** -0.5)
    return (value * below, below + value * density)


def normalize(inputs):
    values = inputs.astype(f32)
    centered = values - jnp.mean(values, axis=-1, keepdims=True)
    rstd = lax.rsqrt(jnp.mean(centered * centered, axis=-1, keepdims=True) + eps)
    return (centered * rstd, rstd)


def norm_back(unit, rstd, dunit, upper):
    inner = (
        dunit
        - jnp.mean(dunit, axis=-1, keepdims=True)
        - unit * jnp.mean(dunit * unit, axis=-1, keepdims=True)
    )
    return (upper.astype(f32) + rstd * inner).astype(bf16)


def shifted(block, axis, distance):
    size = lax.axis_size(axis)
    return lax.ppermute(block, axis, [(i, (i + distance) % size) for i in range(size)])


def scattered(blocks, axis):
    size = lax.axis_size(axis)
    me = lax.axis_index(axis)

    def part(offset):
        return lax.dynamic_index_in_dim(blocks, (me + offset) % size, 0, keepdims=False)

    return [part(0)] + [shifted(part(k), axis, k) for k in range(1, size)]


def sum_of(blocks):
    total = blocks[0].astype(f32)
    for block in blocks[1:]:
        total = total + block.astype(f32)
    return total


def other_core(block):
    size = lax.axis_size("dp")
    return lax.ppermute(block, "dp", [(i, i ^ 1) for i in range(size)])


def next_chip(block, direction):
    size = lax.axis_size("dp")
    return lax.ppermute(block, "dp", [(i, (i + 2 * direction) % size) for i in range(size)])


def from_here(blocks):
    chips = blocks.shape[0]
    chip = lax.axis_index("dp") // 2
    return [
        lax.dynamic_index_in_dim(blocks, (chip + k) % chips, 0, keepdims=False)
        for k in range(chips)
    ]


def passed_on(moving, block, way):
    return next_chip((moving.astype(f32) + block.astype(f32)).astype(bf16), way)


copies = 8


def start_copies(source_ref, out_ref, sems):
    rows = source_ref.shape[0] // copies
    started = []
    for i in range(copies):
        part = pl.ds(i * rows, rows)
        copy = pltpu.make_async_copy(source_ref.at[part], out_ref.at[part], sems.at[i])
        copy.start()
        started.append(copy)
    return started


def fetch_kernel(source_ref, out_ref, sems):
    for copy in start_copies(source_ref, out_ref, sems):
        copy.wait()


def fetched(weight):
    return pl.pallas_call(
        fetch_kernel,
        in_specs=[pl.BlockSpec(memory_space=pltpu.HBM)],
        out_specs=pl.BlockSpec(memory_space=pltpu.VMEM),
        out_shape=pltpu.VMEM(weight.shape, weight.dtype),
        scratch_shapes=[pltpu.SemaphoreType.DMA((copies,))],
        compiler_params=pltpu.CompilerParams(vmem_limit_bytes=1024 * 1024),
        cost_estimate=pl.CostEstimate(
            flops=0, bytes_accessed=4 * weight.size, transcendentals=0
        ),
    )(pltpu.with_memory_space_constraint(weight, pltpu.HBM))


def few_rows_kernel(rows_ref, weight_ref, out_ref, held_ref, sems):
    rows = weight_ref.shape[0] // copies
    total = jnp.zeros(out_ref.shape, f32)
    for i, copy in enumerate(start_copies(weight_ref, held_ref, sems)):
        copy.wait()
        part = pl.ds(i * rows, rows)
        total = total + lax.dot_general(
            rows_ref[part, :],
            held_ref[part, :],
            (((0,), (0,)), ((), ())),
            preferred_element_type=f32,
        )
    out_ref[...] = total


def few_rows_product(rows, weight):
    few, depth = rows.shape
    cols = weight.shape[1]
    padded = jnp.pad(rows, ((0, -few % 16), (0, 0))).T
    vmem = pl.BlockSpec(memory_space=pltpu.VMEM)
    out = pl.pallas_call(
        few_rows_kernel,
        in_specs=[vmem, pl.BlockSpec(memory_space=pltpu.HBM)],
        out_specs=vmem,
        out_shape=jax.ShapeDtypeStruct((padded.shape[1], cols), f32),
        scratch_shapes=[
            pltpu.VMEM(weight.shape, weight.dtype),
            pltpu.SemaphoreType.DMA((copies,)),
        ],
        compiler_params=pltpu.CompilerParams(vmem_limit_bytes=8 * 1024 * 1024),
        cost_estimate=pl.CostEstimate(
            flops=2 * few * weight.size, bytes_accessed=2 * weight.size, transcendentals=0
        ),
    )(padded, pltpu.with_memory_space_constraint(weight, pltpu.HBM))
    return out[:few]


def after(value, *others):
    return lax.optimization_barrier((value, *others))[0]


def tied(*values):
    return lax.optimization_barrier(values)


def columns_of_core(block, core):
    half = block.shape[1] // 2
    return lax.dynamic_slice_in_dim(block, core * half, half, 1)


def rows_of_both(total):
    core = lax.axis_index("dp") % 2
    rows = total.shape[0] // 2
    mine = lax.dynamic_slice_in_dim(total, core * rows, rows, 0)
    theirs = other_core(lax.dynamic_slice_in_dim(total, (1 - core) * rows, rows, 0))
    return jnp.where(
        core == 0,
        jnp.concatenate([mine, theirs], axis=1),
        jnp.concatenate([theirs, mine], axis=1),
    )


def per_device(
    enc_inputs,
    enc_output,
    target_feats,
    pos_table,
    ctx_count,
    tgt_index,
    tgt_count,
    in_proj,
    out_proj,
    up_weight,
    down_weight,
):
    micro, rows, width = enc_output.shape
    slots = tgt_index.shape[1]
    toks = target_feats.shape[1]
    sections = lax.axis_size("section")
    section_idx = lax.axis_index("section")
    shards = lax.axis_size("mp")
    shard_idx = lax.axis_index("mp")
    share = rows // shards
    up_w = up_weight[0]
    down_w = down_weight[0]
    units = up_w.shape[1]

    both_part = jnp.dot(in_proj, out_proj, preferred_element_type=f32).astype(bf16)
    both = lax.all_gather(both_part, "dp", axis=0, tiled=True)
    counts = lax.optimization_barrier(jnp.stack([ctx_count, tgt_count]))
    ctx_count = counts[0]
    tgt_count = counts[1]
    ctx_n = ctx_count.astype(f32)
    tgt_n = tgt_count.astype(f32)
    ctx_live = lax.broadcasted_iota(jnp.int32, (micro, rows), 1) < ctx_count[:, None]
    pooled_sum = jnp.einsum(
        "cr,crd->cd", ctx_live.astype(bf16), enc_output, preferred_element_type=f32
    )
    pooled = (pooled_sum / ctx_n[:, None]).astype(bf16)
    tgt_live = lax.broadcasted_iota(jnp.int32, (micro, slots), 1) < tgt_count[:, None]
    hits = tgt_index[:, :, None] == lax.broadcasted_iota(jnp.int32, (micro, slots, toks), 2)
    picks = jnp.sum(jnp.where(hits & tgt_live[:, :, None], 1.0, 0.0), axis=1).astype(bf16)
    target_mean = (
        jnp.einsum("ct,ctd->cd", picks, target_feats, preferred_element_type=f32) / tgt_n[:, None]
    )
    pos_mean = jnp.dot(picks, pos_table, preferred_element_type=f32) / tgt_n[:, None]
    pos_high = pos_mean.astype(bf16)
    pos_low = (pos_mean - pos_high.astype(f32)).astype(bf16)
    pos_out = jnp.dot(
        jnp.concatenate([pos_high, pos_low]), out_proj, preferred_element_type=f32
    )
    known = pos_out[:micro] + pos_out[micro:] - target_mean
    total = loss_scale * (known + jnp.dot(pooled, both, preferred_element_type=f32))
    dpooled_part = jnp.dot(total.astype(bf16), both.T, preferred_element_type=f32)
    dpooled_parts = [dpooled_part] + [shifted(dpooled_part, "mp", k) for k in range(1, shards)]

    own = micro * share
    inputs = enc_inputs[0].reshape(micro, shards, share, width)
    inputs = inputs.transpose(1, 0, 2, 3).reshape(shards * own, width)
    inputs = lax.optimization_barrier(inputs)
    row_of = jnp.arange(shards)[:, None, None] * share + jnp.arange(share)[None, None, :]
    live = row_of < ctx_count[None, :, None]
    unit_b = normalize(inputs)[0].astype(bf16)
    pre = jnp.dot(unit_b, up_w, preferred_element_type=f32)
    act, slope = gelu_and_slope(pre)
    act = act.astype(bf16)
    slope = slope.astype(bf16)
    dpooled_parts, act, slope = tied(dpooled_parts, act, slope)
    top = (sum_of(dpooled_parts) / ctx_n[:, None]).astype(bf16)
    near = lax.dynamic_slice_in_dim(inputs, shard_idx * own, own, 0)
    near = normalize(lax.optimization_barrier(near))

    core = lax.axis_index("dp") % 2
    upper = jnp.where(live[..., None], top[None, :, None, :], jnp.zeros((), bf16))
    upper = upper.reshape(shards * own, width)
    upper_own = lax.dynamic_slice_in_dim(upper, shard_idx * own, own, 0)
    other_unit = other_core(unit_b)
    last = []
    for step in range(sections - 1):
        if step == 0:
            dact = few_rows_product(top, down_w)
            dact = jnp.where(live[..., None], dact[None, :, None, :], 0.0)
            dact = dact.reshape(shards * own, units)
        else:
            dact = jnp.dot(upper, down_near, preferred_element_type=f32)
        dpre = lax.optimization_barrier((dact * slope).astype(bf16))
        dunit_part = jnp.dot(dpre, up_w.T, preferred_element_type=f32).astype(bf16)
        parts = scattered(dunit_part.reshape(shards, own, width), "mp")
        if step == 0:
            last = [
                jnp.concatenate([unit_b, other_unit]),
                *[columns_of_core(x, c) for x in after((act, slope), dunit_part) for c in (core, 1 - core)],
            ]
        if step == 1:
            last = [last[0], jnp.concatenate(last[1:3]), jnp.concatenate(last[3:5])]
            last = last + [columns_of_core(up_w, core)]
        if step == 2:
            last = last + [columns_of_core(down_w, core)]
        parts, last, near = tied(parts, last, near)
        dx = norm_back(*near, sum_of(parts), upper_own)
        source = sections - 1 - step
        arrived = lax.ppermute(dx, "section", [(source, source - 1)])
        down_near = down_w
        if step == 1:
            down_near = fetched(after(down_w, dx))
            arrived, down_near = tied(arrived, down_near)
        if step == 0:
            last[2] = other_core(last[2])
            last[4] = other_core(last[4])
        upper_own = jnp.where(section_idx == source - 1, arrived, upper_own)
        upper = lax.all_gather(upper_own, "mp", axis=0, tiled=True)
    unit_all, act_all, slope_all, up_half, down_half = last

    chips = lax.axis_size("dp") // 2
    half = chips // 2
    block = (chips, width // chips, units // 2)
    upper_all = lax.optimization_barrier(jnp.concatenate([upper, other_core(upper)]))
    down_part = jnp.einsum("rd,rf->df", upper_all, act_all, preferred_element_type=f32)
    down_blocks = lax.optimization_barrier(from_here(down_part.astype(bf16).reshape(block)))
    dact = jnp.dot(after(upper_all, *down_blocks), down_half, preferred_element_type=f32)
    dpre_all = lax.optimization_barrier((dact * slope_all).astype(bf16))
    up_part = jnp.einsum("rd,rf->df", unit_all, dpre_all, preferred_element_type=f32)
    up_blocks = lax.optimization_barrier(from_here(up_part.astype(bf16).reshape(block)))
    streams = [
        (down_blocks, -1, half),
        (down_blocks, 1, half - 1),
        (up_blocks, 1, half),
        (up_blocks, -1, half - 1),
    ]
    hops = [next_chip(blocks[way * reach], way) for blocks, way, reach in streams]
    hops = list(tied(*hops[:1], up_blocks)[:1]) + hops[1:]
    dpre_all = after(dpre_all, down_blocks, up_blocks)
    dunit_part = jnp.dot(dpre_all, up_half.T, preferred_element_type=f32).astype(bf16)
    dunit_part = dunit_part.reshape(2, shards, own, width)
    before = dunit_part
    dunit_part = (dunit_part[0].astype(f32) + other_core(dunit_part[1]).astype(f32)).astype(bf16)
    for hop in range(1, half):
        for i, (blocks, way, reach) in enumerate(streams):
            if hop < reach:
                moving = after(hops[i], before)
                before = moving.astype(f32) + blocks[way * (reach - hop)].astype(f32)
                before = before.astype(bf16)
                hops[i] = next_chip(before, way)
        if hop == 1:
            parts = scattered(after(dunit_part, before), "mp")
            before = parts[0]
    parts = list(after((*parts,), before))
    dx = norm_back(*near, sum_of(parts), upper_own)
    down_sum = rows_of_both(sum_of([down_blocks[0], hops[0], hops[1]]).astype(bf16))
    up_sum = rows_of_both(sum_of([up_blocks[0], hops[2], hops[3]]).astype(bf16))
    return (up_sum[None], down_sum[None], dx.reshape(1, micro, share, width))


def solution(mesh):
    return jax.shard_map(
        per_device,
        mesh=mesh,
        in_specs=(
            P("section", "dp", None, None),
            P("dp", None, None),
            P("dp", None, "mp"),
            P(),
            P("dp"),
            P("dp", None),
            P("dp"),
            P("dp", None),
            P(None, "mp"),
            P("section", None, "mp"),
            P("section", None, "mp"),
        ),
        out_specs=(
            P("section", "dp", "mp"),
            P("section", "dp", "mp"),
            P("section", "dp", "mp", None),
        ),
        check_vma=False,
    )
```

```python
import jax
import jax.numpy as jnp
from jax import lax
from jax.experimental import pallas as pl
from jax.experimental.pallas import tpu as pltpu
from jax.sharding import PartitionSpec as P

eps = 1e-06
loss_scale = 64.0
f32 = jnp.float32
bf16 = jnp.bfloat16


def gelu_and_slope(value):
    below = 0.5 + 0.5 * lax.erf(value * (0.5**0.5))
    density = jnp.exp(-0.5 * value * value) * ((2.0 * 3.141592653589793) ** -0.5)
    return (value * below, below + value * density)


def normalize(inputs):
    values = inputs.astype(f32)
    centered = values - jnp.mean(values, axis=-1, keepdims=True)
    rstd = lax.rsqrt(jnp.mean(centered * centered, axis=-1, keepdims=True) + eps)
    return (centered * rstd, rstd)


def norm_back(unit, rstd, dunit, upper):
    inner = (
        dunit
        - jnp.mean(dunit, axis=-1, keepdims=True)
        - unit * jnp.mean(dunit * unit, axis=-1, keepdims=True)
    )
    return (upper.astype(f32) + rstd * inner).astype(bf16)


def shifted(block, axis, distance):
    size = lax.axis_size(axis)
    return lax.ppermute(block, axis, [(i, (i + distance) % size) for i in range(size)])


def scattered(blocks, axis):
    size = lax.axis_size(axis)
    me = lax.axis_index(axis)

    def part(offset):
        return lax.dynamic_index_in_dim(blocks, (me + offset) % size, 0, keepdims=False)

    return [part(0)] + [shifted(part(k), axis, k) for k in range(1, size)]


def sum_of(blocks):
    total = blocks[0].astype(f32)
    for block in blocks[1:]:
        total = total + block.astype(f32)
    return total


def other_core(block):
    size = lax.axis_size("dp")
    return lax.ppermute(block, "dp", [(i, i ^ 1) for i in range(size)])


def next_chip(block, direction):
    size = lax.axis_size("dp")
    return lax.ppermute(block, "dp", [(i, (i + 2 * direction) % size) for i in range(size)])


def from_here(blocks):
    chips = blocks.shape[0]
    chip = lax.axis_index("dp") // 2
    return [
        lax.dynamic_index_in_dim(blocks, (chip + k) % chips, 0, keepdims=False)
        for k in range(chips)
    ]


def passed_on(moving, block, way):
    return next_chip((moving.astype(f32) + block.astype(f32)).astype(bf16), way)


copies = 8


def start_copies(source_ref, out_ref, sems):
    rows = source_ref.shape[0] // copies
    started = []
    for i in range(copies):
        part = pl.ds(i * rows, rows)
        copy = pltpu.make_async_copy(source_ref.at[part], out_ref.at[part], sems.at[i])
        copy.start()
        started.append(copy)
    return started


def fetch_kernel(source_ref, out_ref, sems):
    for copy in start_copies(source_ref, out_ref, sems):
        copy.wait()


def fetched(weight):
    return pl.pallas_call(
        fetch_kernel,
        in_specs=[pl.BlockSpec(memory_space=pltpu.HBM)],
        out_specs=pl.BlockSpec(memory_space=pltpu.VMEM),
        out_shape=pltpu.VMEM(weight.shape, weight.dtype),
        scratch_shapes=[pltpu.SemaphoreType.DMA((copies,))],
        compiler_params=pltpu.CompilerParams(vmem_limit_bytes=1024 * 1024),
        cost_estimate=pl.CostEstimate(
            flops=0, bytes_accessed=4 * weight.size, transcendentals=0
        ),
    )(pltpu.with_memory_space_constraint(weight, pltpu.HBM))


def few_rows_kernel(rows_ref, weight_ref, out_ref, held_ref, sems):
    rows = weight_ref.shape[0] // copies
    total = jnp.zeros(out_ref.shape, f32)
    for i, copy in enumerate(start_copies(weight_ref, held_ref, sems)):
        copy.wait()
        part = pl.ds(i * rows, rows)
        total = total + lax.dot_general(
            rows_ref[part, :],
            held_ref[part, :],
            (((0,), (0,)), ((), ())),
            preferred_element_type=f32,
        )
    out_ref[...] = total


def few_rows_product(rows, weight):
    few, depth = rows.shape
    cols = weight.shape[1]
    padded = jnp.pad(rows, ((0, -few % 16), (0, 0))).T
    vmem = pl.BlockSpec(memory_space=pltpu.VMEM)
    out = pl.pallas_call(
        few_rows_kernel,
        in_specs=[vmem, pl.BlockSpec(memory_space=pltpu.HBM)],
        out_specs=vmem,
        out_shape=jax.ShapeDtypeStruct((padded.shape[1], cols), f32),
        scratch_shapes=[
            pltpu.VMEM(weight.shape, weight.dtype),
            pltpu.SemaphoreType.DMA((copies,)),
        ],
        compiler_params=pltpu.CompilerParams(vmem_limit_bytes=8 * 1024 * 1024),
        cost_estimate=pl.CostEstimate(
            flops=2 * few * weight.size, bytes_accessed=2 * weight.size, transcendentals=0
        ),
    )(padded, pltpu.with_memory_space_constraint(weight, pltpu.HBM))
    return out[:few]


def after(value, *others):
    return lax.optimization_barrier((value, *others))[0]


def tied(*values):
    return lax.optimization_barrier(values)


def columns_of_core(block, core):
    half = block.shape[1] // 2
    return lax.dynamic_slice_in_dim(block, core * half, half, 1)


def rows_of_both(total):
    core = lax.axis_index("dp") % 2
    rows = total.shape[0] // 2
    mine = lax.dynamic_slice_in_dim(total, core * rows, rows, 0)
    theirs = other_core(lax.dynamic_slice_in_dim(total, (1 - core) * rows, rows, 0))
    return jnp.where(
        core == 0,
        jnp.concatenate([mine, theirs], axis=1),
        jnp.concatenate([theirs, mine], axis=1),
    )


def per_device(
    enc_inputs,
    enc_output,
    target_feats,
    pos_table,
    ctx_count,
    tgt_index,
    tgt_count,
    in_proj,
    out_proj,
    up_weight,
    down_weight,
):
    micro, rows, width = enc_output.shape
    slots = tgt_index.shape[1]
    toks = target_feats.shape[1]
    sections = lax.axis_size("section")
    section_idx = lax.axis_index("section")
    shards = lax.axis_size("mp")
    shard_idx = lax.axis_index("mp")
    share = rows // shards
    up_w = up_weight[0]
    down_w = down_weight[0]
    units = up_w.shape[1]

    both_part = jnp.dot(in_proj, out_proj, preferred_element_type=f32).astype(bf16)
    both = lax.all_gather(both_part, "dp", axis=0, tiled=True)
    counts = lax.optimization_barrier(jnp.stack([ctx_count, tgt_count]))
    ctx_count = counts[0]
    tgt_count = counts[1]
    ctx_n = ctx_count.astype(f32)
    tgt_n = tgt_count.astype(f32)
    ctx_live = lax.broadcasted_iota(jnp.int32, (micro, rows), 1) < ctx_count[:, None]
    pooled_sum = jnp.einsum(
        "cr,crd->cd", ctx_live.astype(bf16), enc_output, preferred_element_type=f32
    )
    pooled = (pooled_sum / ctx_n[:, None]).astype(bf16)
    tgt_live = lax.broadcasted_iota(jnp.int32, (micro, slots), 1) < tgt_count[:, None]
    hits = tgt_index[:, :, None] == lax.broadcasted_iota(jnp.int32, (micro, slots, toks), 2)
    picks = jnp.sum(jnp.where(hits & tgt_live[:, :, None], 1.0, 0.0), axis=1).astype(bf16)
    target_mean = (
        jnp.einsum("ct,ctd->cd", picks, target_feats, preferred_element_type=f32) / tgt_n[:, None]
    )
    pos_mean = jnp.dot(picks, pos_table, preferred_element_type=f32) / tgt_n[:, None]
    pos_high = pos_mean.astype(bf16)
    pos_low = (pos_mean - pos_high.astype(f32)).astype(bf16)
    pos_out = jnp.dot(
        jnp.concatenate([pos_high, pos_low]), out_proj, preferred_element_type=f32
    )
    known = pos_out[:micro] + pos_out[micro:] - target_mean
    total = loss_scale * (known + jnp.dot(pooled, both, preferred_element_type=f32))
    dpooled_part = jnp.dot(total.astype(bf16), both.T, preferred_element_type=f32)
    dpooled_parts = [dpooled_part] + [shifted(dpooled_part, "mp", k) for k in range(1, shards)]

    own = micro * share
    inputs = enc_inputs[0].reshape(micro, shards, share, width)
    inputs = inputs.transpose(1, 0, 2, 3).reshape(shards * own, width)
    inputs = lax.optimization_barrier(inputs)
    row_of = jnp.arange(shards)[:, None, None] * share + jnp.arange(share)[None, None, :]
    live = row_of < ctx_count[None, :, None]
    unit_b = normalize(inputs)[0].astype(bf16)
    pre = jnp.dot(unit_b, up_w, preferred_element_type=f32)
    act, slope = gelu_and_slope(pre)
    act = act.astype(bf16)
    slope = slope.astype(bf16)
    dpooled_parts, act, slope = tied(dpooled_parts, act, slope)
    top = (sum_of(dpooled_parts) / ctx_n[:, None]).astype(bf16)
    near = lax.dynamic_slice_in_dim(inputs, shard_idx * own, own, 0)
    near = normalize(lax.optimization_barrier(near))

    core = lax.axis_index("dp") % 2
    upper = jnp.where(live[..., None], top[None, :, None, :], jnp.zeros((), bf16))
    upper = upper.reshape(shards * own, width)
    upper_own = lax.dynamic_slice_in_dim(upper, shard_idx * own, own, 0)
    other_unit = other_core(unit_b)
    last = []
    for step in range(sections - 1):
        if step == 0:
            dact = few_rows_product(top, down_w)
            dact = jnp.where(live[..., None], dact[None, :, None, :], 0.0)
            dact = dact.reshape(shards * own, units)
        else:
            dact = jnp.dot(upper, down_near, preferred_element_type=f32)
        dpre = lax.optimization_barrier((dact * slope).astype(bf16))
        dunit_part = jnp.dot(dpre, up_w.T, preferred_element_type=f32).astype(bf16)
        parts = scattered(dunit_part.reshape(shards, own, width), "mp")
        if step == 0:
            last = [
                jnp.concatenate([unit_b, other_unit]),
                *[columns_of_core(x, c) for x in after((act, slope), dunit_part) for c in (core, 1 - core)],
            ]
        if step == 1:
            last = [last[0], jnp.concatenate(last[1:3]), jnp.concatenate(last[3:5])]
            last = last + [columns_of_core(up_w, core)]
        if step == 2:
            last = last + [columns_of_core(down_w, core)]
        parts, last, near = tied(parts, last, near)
        dx = norm_back(*near, sum_of(parts), upper_own)
        source = sections - 1 - step
        arrived = lax.ppermute(dx, "section", [(source, source - 1)])
        down_near = down_w
        if step == 1:
            down_near = fetched(after(down_w, dx))
            arrived, down_near = tied(arrived, down_near)
        if step == 0:
            last[2] = other_core(last[2])
            last[4] = other_core(last[4])
        upper_own = jnp.where(section_idx == source - 1, arrived, upper_own)
        upper = lax.all_gather(upper_own, "mp", axis=0, tiled=True)
    unit_all, act_all, slope_all, up_half, down_half = last

    chips = lax.axis_size("dp") // 2
    half = chips // 2
    block = (chips, width // chips, units // 2)
    near_rows = shards * own
    down_own = jnp.einsum("rd,rf->df", upper, act_all[:near_rows], preferred_element_type=f32)
    dact = jnp.dot(upper, down_half, preferred_element_type=f32)
    upper_other, down_own, dpre_own = tied(
        other_core(upper),
        down_own.astype(bf16),
        (dact * slope_all[:near_rows]).astype(bf16),
    )
    down_part = jnp.einsum("rd,rf->df", upper_other, act_all[near_rows:], preferred_element_type=f32)
    down_part = down_part + down_own.astype(f32)
    down_blocks = lax.optimization_barrier(from_here(down_part.astype(bf16).reshape(block)))
    dact = jnp.dot(after(upper_other, *down_blocks), down_half, preferred_element_type=f32)
    dpre_other = (dact * slope_all[near_rows:]).astype(bf16)
    dpre_all = lax.optimization_barrier(jnp.concatenate([dpre_own, dpre_other]))
    up_part = jnp.einsum("rd,rf->df", unit_all, dpre_all, preferred_element_type=f32)
    up_blocks = lax.optimization_barrier(from_here(up_part.astype(bf16).reshape(block)))
    streams = [
        (down_blocks, -1, half),
        (down_blocks, 1, half - 1),
        (up_blocks, 1, half),
        (up_blocks, -1, half - 1),
    ]
    hops = [next_chip(blocks[way * reach], way) for blocks, way, reach in streams]
    hops = list(tied(*hops[:1], up_blocks)[:1]) + hops[1:]
    dpre_all = after(dpre_all, down_blocks, up_blocks)
    dunit_part = jnp.dot(dpre_all, up_half.T, preferred_element_type=f32).astype(bf16)
    dunit_part = dunit_part.reshape(2, shards, own, width)
    before = dunit_part
    dunit_part = (dunit_part[0].astype(f32) + other_core(dunit_part[1]).astype(f32)).astype(bf16)
    for hop in range(1, half):
        for i, (blocks, way, reach) in enumerate(streams):
            if hop < reach:
                moving = after(hops[i], before)
                before = moving.astype(f32) + blocks[way * (reach - hop)].astype(f32)
                before = before.astype(bf16)
                hops[i] = next_chip(before, way)
        if hop == 1:
            parts = scattered(after(dunit_part, before), "mp")
            before = parts[0]
    parts = list(after((*parts,), before))
    dx = norm_back(*near, sum_of(parts), upper_own)
    down_sum = rows_of_both(sum_of([down_blocks[0], hops[0], hops[1]]).astype(bf16))
    up_sum = rows_of_both(sum_of([up_blocks[0], hops[2], hops[3]]).astype(bf16))
    return (up_sum[None], down_sum[None], dx.reshape(1, micro, share, width))


def solution(mesh):
    return jax.shard_map(
        per_device,
        mesh=mesh,
        in_specs=(
            P("section", "dp", None, None),
            P("dp", None, None),
            P("dp", None, "mp"),
            P(),
            P("dp"),
            P("dp", None),
            P("dp"),
            P("dp", None),
            P(None, "mp"),
            P("section", None, "mp"),
            P("section", None, "mp"),
        ),
        out_specs=(
            P("section", "dp", "mp"),
            P("section", "dp", "mp"),
            P("section", "dp", "mp", None),
        ),
        check_vma=False,
    )
```
